32 devices in a mesh: groups: 1, expert: 16 (over z, y, x), replica: 2 (over core).
Axes of the slice: x: 2, y: 2, z: 4, core: 2. Of those that a mesh axis runs over, the one named last changes fastest.
Arguments:
- hidden_rows: bfloat16 [1024, 3584], P(('groups', 'expert', 'replica')), may hold values from -6 to 6
- norm_gain: float32 [3584], replicated, may hold values from 0.5 to 1.5
- expert_ids: int32 [1024, 2], P(('groups', 'expert', 'replica')), may hold values from 0 to 3, all different within a row; in each aligned block of 32 rows (0 to 31, 32 to 63, ...) at most 32 rows name the same one
- capacity: int32 [4], replicated, may hold values from 16 to 32
- route_probs: float32 [1024, 2], P(('groups', 'expert', 'replica')), may hold values from 0.2 to 1
- w_gate: bfloat16 [16, 2, 3584, 304], P('expert', 'replica'), may hold values from -0.09375 to 0.09375
- w_up: bfloat16 [16, 2, 3584, 304], P('expert', 'replica'), may hold values from -0.09375 to 0.09375
- w_down: bfloat16 [16, 2, 304, 3584], P('expert', 'replica'), may hold values from -0.125 to 0.125
Outputs:
- moved: bfloat16 [1024, 3584], P(('groups', 'expert', 'replica'))
The draws below stay inside these ranges and needn't reach their ends.
Inputs may be any that keep to these rules, and one draw needn't show every extreme that they name: `expert_ids`: in the 8 rows of one device no expert is named more than 32 times, a bound that some block reaches; the two ids of a row differ.
All inputs are finite; a program needn't handle non-finite values.
Results may differ from the reference program's by a relative error of at most 0.006.
Values may be sent and summed in bfloat16 or wider, within the bound.
A program may use at most 64 MiB of HBM per device.

```python
import math
import jax
import jax.numpy as jnp
import numpy as np
from jax import lax

D = 3584
FFE = 2432
TGROUP = 8
ROWS = 32
UNITS = 304
EXPERTS = 4
CAP = 32
TOKENS = 1024
N_EXPERT = 16
N_REPLICA = 2


def set_ends(array, own_key, low, high):
    shape = array.shape
    spot = [jax.random.randint(jax.random.fold_in(own_key, axis), (), 0, shape[axis]) for axis in range(len(shape))]
    array = array.at[tuple(spot)].set(low)
    longest = shape.index(max(shape))
    spot[longest] = (spot[longest] + 1) % shape[longest]
    return array.at[tuple(spot)].set(high)


def level_of(key, extent, pieces, smallest, high):
    def one(position, blocks):
        draws = jax.random.uniform(jax.random.fold_in(jax.random.fold_in(key, 6), position), (blocks,), jnp.float32, smallest / len(pieces), high / len(pieces))
        return jnp.repeat(jnp.exp(draws), extent[position] // blocks).reshape((-1,) + (1,) * (len(extent) - position - 1))

    factor_of = one(*pieces[0])
    for cut in pieces[1:]:
        factor_of = factor_of * one(*cut)
    return factor_of


def shared_out(own_key, own, number, rows, amount, top, bound, lean):
    order = jax.random.permutation(own_key, amount)
    crowded, usual = shares(amount, rows * top, bound, lean, True), shares(amount, rows * top, bound, lean, False)
    places = jnp.arange(amount)

    def named(lengths, offset_by):
        used = int((lengths > 0).sum())
        fixed = max(1, used // 4)
        shifted = fixed + (places - fixed + offset_by * (used - fixed)) % max(1, amount - fixed)
        return jnp.zeros((amount,), jnp.int32).at[order[jnp.where(places < fixed, places, shifted)]].set(jnp.asarray(lengths, jnp.int32))

    lengths = jnp.where(number % 4 == 0, named(crowded, number // 4), named(usual, number - number // 4 - 1))
    mixed = jax.random.permutation(jax.random.fold_in(own, 3), amount)
    donor, sink = mixed[0:amount // 2 * 2:2], mixed[1:amount // 2 * 2:2]
    room = jnp.minimum(lengths[donor] - 1, bound - lengths[sink]) // 2
    room = jnp.where((donor == order[0]) | (sink == order[0]) | (lengths[sink] == 0), 0, jnp.maximum(room, 0))
    shifted = jax.random.randint(jax.random.fold_in(own, 4), (amount // 2,), 0, 1 << 20) % (room + 1)
    lengths = lengths.at[donor].add(-shifted).at[sink].add(shifted)
    members = jnp.searchsorted(jnp.cumsum(lengths), jnp.arange(rows * top), side="right").astype(jnp.int32)
    table = members.reshape(top, rows).T
    table = table[jax.random.permutation(jax.random.fold_in(own, 1), rows)]
    offset_by = jax.random.randint(jax.random.fold_in(own, 2), (rows, 1), 0, top)
    return jnp.take_along_axis(table, (jnp.arange(top)[None, :] + offset_by) % top, axis=1)


def shares(count, total, bound, lean, full):
    loads = [(1 << 20) // math.isqrt(standing ** lean) + 1 for standing in range(1, count + 1)]
    largest = bound if full else min(bound, max(-(-total // count), total * loads[0] // sum(loads)))
    least = 1 if total - largest >= count - 1 else 0
    counts, rest = [largest] + [least] * (count - 1), total - largest - least * (count - 1)
    while rest > 0:
        candidates = [i for i in range(1, count) if counts[i] < largest] or [i for i in range(1, count) if counts[i] < bound]
        mass, remaining = sum([loads[i] for i in candidates]), rest
        for i in candidates:
            extra = min(bound - counts[i], max(1, remaining * loads[i] // mass), rest)
            counts[i] = counts[i] + extra
            rest = rest - extra
    return np.array(counts)


def centred(rng, dims, deviation, reach, shards=(), held_as=jnp.bfloat16):
    array = deviation * jax.random.normal(rng, dims, jnp.float32)
    if shards:
        array = array * level_of(rng, dims, shards, -0.22, 0.18)
    return jnp.clip(array, -reach, reach).astype(held_as)


def setup_inputs(seed: int = 0, part: int = 0) -> dict:
    keys = jax.random.split(jax.random.key(seed), 9)
    own_keys = jax.random.split(jax.random.fold_in(keys[8], part), 9)
    hidden_rows = centred(own_keys[0], (TOKENS, D), 1.0, 6.0, ((0, 32),))
    norm_gain = jnp.clip(1.0 + 0.1 * jax.random.normal(keys[1], (D,), jnp.float32), 0.5, 1.5)
    expert_ids_keys = jax.random.split(jax.random.fold_in(own_keys[2], 1), TOKENS // ROWS)
    expert_ids_turns = jax.random.permutation(jax.random.fold_in(own_keys[2], 3), TOKENS // ROWS)
    expert_ids = jax.vmap(lambda own, number: shared_out(jax.random.fold_in(own_keys[2], 2), own, number, ROWS, EXPERTS, 2, CAP, 2))(expert_ids_keys, expert_ids_turns).reshape((TOKENS, 2))
    capacity = set_ends(jax.random.randint(keys[3], (EXPERTS,), max(1, CAP // 2), CAP + 1), jax.random.fold_in(keys[3], 1), max(1, CAP // 2), CAP).astype(jnp.int32)
    route_probs = jnp.clip(0.2 + 0.8 * jax.random.uniform(own_keys[4], (TOKENS, 2), jnp.float32) ** level_of(own_keys[4], (TOKENS, 2), ((0, 32),), -0.2, 0.2), 0.2, 1.0)
    w_gate = centred(keys[5], (N_EXPERT, N_REPLICA, D, UNITS), D ** -0.5, 0.09375, ((0, 16), (1, 2)))
    w_up = centred(keys[6], (N_EXPERT, N_REPLICA, D, UNITS), D ** -0.5, 0.09375, ((0, 16), (1, 2)))
    w_down = centred(keys[7], (N_EXPERT, N_REPLICA, UNITS, D), FFE ** -0.5, 0.125, ((0, 16), (1, 2)))
    return dict(hidden_rows=hidden_rows, norm_gain=norm_gain, expert_ids=expert_ids, capacity=capacity, route_probs=route_probs, w_gate=w_gate, w_up=w_up, w_down=w_down)


def reference(hidden_rows, norm_gain, expert_ids, capacity, route_probs, w_gate, w_up, w_down):
    widened = hidden_rows.astype(jnp.float32)
    scaling = lax.rsqrt(lax.optimization_barrier(jnp.mean(widened * widened, axis=-1, keepdims=True)) + 1e-05)
    normed = (widened * scaling * norm_gain).astype(jnp.bfloat16)
    blocks = TOKENS // ROWS
    assigned = expert_ids.reshape(blocks, 2 * ROWS)
    labels = jnp.arange(EXPERTS, dtype=jnp.int32)
    onehot = (assigned[:, :, None] == labels[None, None, :]).astype(jnp.int32)
    earlier = jnp.cumsum(onehot, axis=1) - onehot
    slot_rank = lax.optimization_barrier(jnp.sum(earlier * onehot, axis=2))
    cap_limit = lax.optimization_barrier(jnp.sum(onehot * capacity[None, None, :], axis=2))
    keep_mask = (slot_rank < cap_limit).astype(jnp.int32)
    route_w = route_probs.reshape(blocks, 2 * ROWS).astype(jnp.float32)
    slot_iota = jnp.arange(CAP, dtype=jnp.int32)
    rows_assign = jnp.repeat(normed.reshape(blocks, ROWS, D), 2, axis=1).astype(jnp.float32)
    families = N_EXPERT // TGROUP
    gates = w_gate.reshape(families, TGROUP, N_REPLICA, D, UNITS).transpose(0, 2, 1, 3, 4).reshape(EXPERTS, TGROUP, D, UNITS)
    ups = w_up.reshape(families, TGROUP, N_REPLICA, D, UNITS).transpose(0, 2, 1, 3, 4).reshape(EXPERTS, TGROUP, D, UNITS)
    downs = w_down.reshape(families, TGROUP, N_REPLICA, UNITS, D).transpose(0, 2, 1, 3, 4).reshape(EXPERTS, TGROUP, UNITS, D)

    def one_expert(running, inputs):
        expert_label, w_gate_e, w_up_e, w_down_e = inputs
        chosen = (assigned == expert_label).astype(jnp.int32) * keep_mask
        select = (chosen[:, None, :] * (slot_rank[:, None, :] == slot_iota[None, :, None]).astype(jnp.int32)).astype(jnp.float32)
        picked = jnp.einsum('bcs,bsd->bcd', select, rows_assign).astype(jnp.bfloat16).reshape(blocks * CAP, D)
        result = jnp.zeros((blocks * CAP, D), jnp.float32)
        for member in range(TGROUP):
            gate_out = jnp.dot(picked, w_gate_e[member], preferred_element_type=jnp.float32)
            up_out = jnp.dot(picked, w_up_e[member], preferred_element_type=jnp.float32)
            hidden = (jax.nn.silu(gate_out) * up_out).astype(jnp.bfloat16)
            piece = jnp.dot(hidden, w_down_e[member], preferred_element_type=jnp.float32).astype(jnp.bfloat16)
            piece = lax.optimization_barrier(piece)
            result = result + piece.astype(jnp.float32)
        weighted = select * route_w[:, None, :]
        returned_rows = jnp.einsum('bcs,bcd->bsd', weighted, result.reshape(blocks, CAP, D))
        return (running + returned_rows, None)
    start = jnp.zeros((blocks, 2 * ROWS, D), jnp.float32)
    running, _ = lax.scan(one_expert, start, (labels, gates, ups, downs))
    mixture = running.reshape(blocks, ROWS, 2, D).sum(axis=2).reshape(TOKENS, D)
    return (widened + mixture).astype(jnp.bfloat16)
```

```python
import jax
import jax.numpy as jnp
from jax import lax
from jax.experimental import pallas as pl
from jax.experimental.pallas import tpu as pltpu
from jax.sharding import PartitionSpec as P

TGROUP = 8


def serve_slots(received, w_gate, w_up, w_down):
    sources, count, model_width = received.shape
    flattened = received.reshape(sources * count, model_width)
    gate_out = jnp.dot(flattened, w_gate[0, 0], preferred_element_type=jnp.float32)
    up_out = jnp.dot(flattened, w_up[0, 0], preferred_element_type=jnp.float32)
    hidden = (jax.nn.silu(gate_out) * up_out).astype(jnp.bfloat16)
    pieces = jnp.dot(hidden, w_down[0, 0], preferred_element_type=jnp.float32).astype(jnp.bfloat16)
    return pieces.reshape(sources, count, model_width)


def per_device(hidden_rows, norm_gain, expert_ids, capacity, route_probs, w_gate, w_up, w_down):
    row_count, model_width = hidden_rows.shape
    lane_count = lax.axis_size("expert")
    copies = lax.axis_size("replica")
    families = lane_count // TGROUP
    experts = families * copies
    slot_count = min(row_count, max(TGROUP, 4 * row_count // experts))
    widened = hidden_rows.astype(jnp.float32)
    scaling = lax.rsqrt(jnp.mean(widened * widened, axis=-1, keepdims=True) + 1e-05)
    normed = (widened * scaling * norm_gain).astype(jnp.bfloat16)
    assigned = expert_ids.reshape(2 * row_count)
    labels = jnp.arange(experts, dtype=jnp.int32)
    onehot = (assigned[:, None] == labels[None, :]).astype(jnp.int32)
    order_iota = jnp.arange(2 * row_count, dtype=jnp.int32)
    earlier = (order_iota[None, :] < order_iota[:, None]).astype(jnp.float32)
    counted = jnp.dot(earlier, onehot.astype(jnp.float32), preferred_element_type=jnp.float32)
    slot_rank = jnp.sum(counted.astype(jnp.int32) * onehot, axis=1)
    cap_limit = jnp.sum(onehot * capacity[None, :], axis=1)
    keep_mask = (slot_rank < cap_limit).astype(jnp.int32)
    slot_iota = jnp.arange(slot_count, dtype=jnp.int32)
    chosen = onehot.T * keep_mask[None, :]
    selection = chosen[:, None, :] * (slot_rank[None, None, :] == slot_iota[None, :, None]).astype(
        jnp.int32
    )
    selection = selection.astype(jnp.float32).reshape(experts, slot_count, row_count, 2)
    sel_rows = jnp.sum(selection, axis=3)
    weights_rows = jnp.sum(selection * route_probs[None, None, :, :], axis=3)
    outgoing = jnp.einsum(
        "ecr,rd->ecd", sel_rows.astype(jnp.bfloat16), normed, preferred_element_type=jnp.float32
    ).astype(jnp.bfloat16)
    spread = jnp.broadcast_to(
        outgoing.reshape(families, 1, copies, slot_count, model_width),
        (families, TGROUP, copies, slot_count, model_width),
    ).reshape(lane_count * copies, slot_count, model_width)
    pieces = serve_slots(
        lax.all_to_all(spread, ("expert", "replica"), split_axis=0, concat_axis=0, tiled=True),
        w_gate,
        w_up,
        w_down,
    )
    returned = lax.all_to_all(
        pieces, ("expert", "replica"), split_axis=0, concat_axis=0, tiled=True
    )
    summed = (
        returned.reshape(families, TGROUP, copies, slot_count, model_width)
        .astype(jnp.float32)
        .sum(axis=1)
        .reshape(experts, slot_count, model_width)
    )
    mixture = jnp.einsum("ecr,ecd->rd", weights_rows, summed)
    return (widened + mixture).astype(jnp.bfloat16)


CHAIN = 4
LANES = 128
HALF = 16
BLOCK = 2 * HALF
SIDE = CHAIN * BLOCK
BATCH = 2 * SIDE
STEP = 512


def rows_at(dc, dz, h=None):
    start = dc * SIDE + dz * BLOCK
    return pl.ds(start, BLOCK) if h is None else pl.ds(start + h * HALF, HALF)


def layer_kernel(
    hidden_ref, gain_ref, ids_ref, cap_ref, probs_ref, wg_hbm, wu_hbm, wd_hbm, out_ref,
    rows_buf, part_buf, pair_buf, far_buf, near_buf, chain_buf, wg, wu, wd, acc_g, acc_u, hid,
    load_sem, send_sem, recv_sem,
):
    width = hidden_ref.shape[1]
    experts = cap_ref.shape[0]
    me = lax.axis_index("expert")
    core = lax.axis_index("replica")
    total = lax.axis_size("expert")
    x_side = {"expert": me + 1 - 2 * lax.rem(me, 2)}
    y_side = {"expert": me + 2 - 4 * lax.rem(lax.div(me, 2), 2)}
    sibling = {"replica": 1 - core}
    along = [{"expert": lax.rem(me + 4 * k, total)} for k in range(CHAIN)]
    near = (x_side, y_side)
    far = (y_side, x_side)

    loads = [
        pltpu.make_async_copy(src, dst, load_sem.at[n])
        for n, (src, dst) in enumerate(((wg_hbm, wg), (wu_hbm, wu), (wd_hbm, wd)))
    ]
    for load in loads:
        load.start()

    barrier = pltpu.get_barrier_semaphore()
    partners = [x_side, y_side, sibling] + along[1:]
    for partner in partners:
        pl.semaphore_signal(barrier, inc=1, device_id=partner, device_id_type=pl.DeviceIdType.MESH)

    widened = hidden_ref[...].astype(jnp.float32)
    scaling = lax.rsqrt(jnp.mean(widened * widened, axis=-1, keepdims=True) + 1e-05)
    rows_buf[0, pl.ds(0, BLOCK), pl.ds(0, width)] = (widened * scaling * gain_ref[...]).astype(jnp.bfloat16)
    lane = lax.broadcasted_iota(jnp.int32, (BLOCK, LANES), 1)
    label = jnp.where(lane < LANES // 2, lane, lane - LANES // 2)
    first = ids_ref[:, 0:1] == label
    second = ids_ref[:, 1:2] == label
    named = jnp.where(first | second, 1.0, 0.0)
    earlier = lax.broadcasted_iota(jnp.int32, (BLOCK, BLOCK), 1) < lax.broadcasted_iota(jnp.int32, (BLOCK, BLOCK), 0)
    rank = jnp.dot(
        jnp.where(earlier, 1.0, 0.0).astype(jnp.bfloat16),
        named.astype(jnp.bfloat16),
        preferred_element_type=jnp.float32,
    )
    limit = jnp.zeros((BLOCK, LANES), jnp.float32)
    for e in range(experts):
        limit = jnp.where(label == e, cap_ref[e].astype(jnp.float32), limit)
    weight = jnp.where(first, probs_ref[:, 0:1], 0.0) + jnp.where(second, probs_ref[:, 1:2], 0.0)
    weight = jnp.where(rank < limit, weight, 0.0)
    high = weight.astype(jnp.bfloat16).astype(jnp.float32)
    rows_buf[0, pl.ds(0, BLOCK), pl.ds(width, LANES)] = jnp.where(
        lane < LANES // 2, high, weight - high
    ).astype(jnp.bfloat16)

    pl.semaphore_wait(barrier, len(partners))

    sent = {}

    def send(name, src, dst, device):
        n = len(sent)
        copy = pltpu.make_async_remote_copy(
            src_ref=src, dst_ref=dst, send_sem=send_sem.at[n], recv_sem=recv_sem.at[n],
            device_id=device, device_id_type=pl.DeviceIdType.MESH,
        )
        copy.start()
        sent[name] = copy

    def to_near(dz):
        for h in range(2):
            send(("near", dz, h), rows_buf.at[0, rows_at(0, dz, h)], rows_buf.at[1, rows_at(0, dz, h)], near[h])

    def to_far(b, dz):
        for h in range(2):
            send(("far", b, dz, h), rows_buf.at[b, rows_at(0, dz, h)], rows_buf.at[2 + b, rows_at(0, dz, h)], far[h])

    def to_sibling(batch, dz):
        send(("pair", batch, dz), rows_buf.at[batch, rows_at(0, dz)], rows_buf.at[batch, rows_at(1, dz)], sibling)

    def got(*name):
        sent[name].wait_recv()

    for k in (1, 3, 2):
        send(("along", k), rows_buf.at[0, rows_at(0, 0)], rows_buf.at[0, rows_at(0, CHAIN - k)], along[k])
    to_near(0)
    to_far(0, 0)
    to_sibling(0, 0)

    def relay_along(dz):
        got("along", CHAIN - dz)
        to_near(dz)
        to_far(0, dz)
        to_sibling(0, dz)

    def relay_near(dz):
        got("near", dz, 0)
        got("near", dz, 1)
        to_far(1, dz)
        to_sibling(1, dz)

    def relay_far(b, dz):
        got("far", b, dz, 0)
        got("far", b, dz, 1)
        to_sibling(2 + b, dz)

    def compute(batch):
        for dz in range(CHAIN):
            got("pair", batch, dz)
        acc_g[...] = jnp.zeros_like(acc_g)
        acc_u[...] = jnp.zeros_like(acc_u)

        def project(n, carry):
            at = pl.ds(pl.multiple_of(n * STEP, STEP), STEP)
            block = rows_buf[batch, :, at]
            acc_g[...] += jnp.dot(block, wg[at, :], preferred_element_type=jnp.float32)
            acc_u[...] += jnp.dot(block, wu[at, :], preferred_element_type=jnp.float32)
            return carry

        lax.fori_loop(0, width // STEP, project, 0)
        gate = acc_g[...]
        hid[...] = (jax.nn.silu(gate) * acc_u[...]).astype(jnp.bfloat16)
        mine = lax.div(me, TGROUP) * 2 + core
        lanes = lax.broadcasted_iota(jnp.int32, (BATCH, LANES), 1)
        chosen = (lanes == mine) | (lanes == mine + LANES // 2)
        tail = rows_buf[batch, :, pl.ds(width, LANES)].astype(jnp.float32)
        combine = jnp.sum(jnp.where(chosen, tail, 0.0), axis=1, keepdims=True)

        def expand(n, carry):
            at = pl.ds(pl.multiple_of(n * STEP, STEP), STEP)
            piece = jnp.dot(hid[...], wd[:, at], preferred_element_type=jnp.float32)
            part_buf[batch, :, at] = (piece * combine).astype(jnp.bfloat16)
            return carry

        lax.fori_loop(0, width // STEP, expand, 0)
        send(("sum", batch), part_buf.at[batch, pl.ds(SIDE, SIDE)], pair_buf.at[batch], sibling)

    def add_rows(batch, dst, src_ref, count):
        def body(n, carry):
            at = pl.ds(pl.multiple_of(n * HALF, HALF), HALF)
            to = pl.ds(pl.multiple_of(dst + n * HALF, HALF), HALF)
            part_buf[batch, to, :] = (
                part_buf[batch, to, :].astype(jnp.float32) + src_ref[at, :].astype(jnp.float32)
            ).astype(jnp.bfloat16)
            return carry

        lax.fori_loop(0, count, body, 0)

    def sum_pair(batch):
        got("sum", batch)
        add_rows(batch, 0, pair_buf.at[batch], SIDE // HALF)

    relay_along(1)
    relay_near(0)
    relay_along(3)
    relay_near(1)
    relay_along(2)
    relay_near(3)
    relay_near(2)
    for load in loads:
        load.wait()
    compute(0)
    compute(1)
    for dz in (0, 1, 3, 2):
        relay_far(0, dz)
    compute(2)
    for dz in (0, 1, 3, 2):
        relay_far(1, dz)
    sum_pair(2)

    def back_far(b):
        for dz in (2, 1, 3, 0):
            for h in range(2):
                send(
                    ("back_far", b, dz, h), part_buf.at[2 + b, rows_at(0, dz, h)],
                    far_buf.at[b, rows_at(0, dz, h)], far[h],
                )

    back_far(0)
    compute(3)
    sum_pair(0)
    sum_pair(1)
    sum_pair(3)
    back_far(1)
    for b in (0, 1):
        for dz in (2, 1, 3, 0):
            got("back_far", b, dz, 0)
            got("back_far", b, dz, 1)
            add_rows(b, dz * BLOCK, far_buf.at[b, rows_at(0, dz)], 2)
            if b == 1:
                for h in range(2):
                    send(
                        ("back_near", dz, h), part_buf.at[1, rows_at(0, dz, h)],
                        near_buf.at[rows_at(0, dz, h)], near[h],
                    )
    for dz in (2, 1, 3, 0):
        got("back_near", dz, 0)
        got("back_near", dz, 1)
        add_rows(0, dz * BLOCK, near_buf.at[rows_at(0, dz)], 2)
        if dz:
            send(("home", dz), part_buf.at[0, rows_at(0, dz)], chain_buf.at[dz - 1], along[dz])
    for dz in (1, 3, 2):
        got("home", dz)
    mixture = part_buf[0, pl.ds(0, BLOCK), :].astype(jnp.float32)
    for dz in range(1, CHAIN):
        mixture = mixture + chain_buf[dz - 1].astype(jnp.float32)
    out_ref[...] = (hidden_ref[...].astype(jnp.float32) + mixture).astype(jnp.bfloat16)
    for copy in sent.values():
        copy.wait_send()


COPIES = 80


def per_device_kernel(hidden_rows, norm_gain, expert_ids, capacity, route_probs, w_gate, w_up, w_down):
    row_count, width = hidden_rows.shape
    units = w_gate.shape[-1]
    vmem = pl.BlockSpec(memory_space=pltpu.VMEM)
    anywhere = pl.BlockSpec(memory_space=pl.ANY)
    bf16 = jnp.bfloat16
    return pl.pallas_call(
        layer_kernel,
        out_shape=jax.ShapeDtypeStruct((row_count, width), bf16),
        in_specs=[vmem, vmem, vmem, pl.BlockSpec(memory_space=pltpu.SMEM), vmem, anywhere, anywhere, anywhere],
        out_specs=vmem,
        scratch_shapes=[
            pltpu.VMEM((4, BATCH, width + LANES), bf16),
            pltpu.VMEM((4, BATCH, width), bf16),
            pltpu.VMEM((4, SIDE, width), bf16),
            pltpu.VMEM((2, SIDE, width), bf16),
            pltpu.VMEM((SIDE, width), bf16),
            pltpu.VMEM((CHAIN - 1, BLOCK, width), bf16),
            pltpu.VMEM((width, units), bf16),
            pltpu.VMEM((width, units), bf16),
            pltpu.VMEM((units, width), bf16),
            pltpu.VMEM((BATCH, units), jnp.float32),
            pltpu.VMEM((BATCH, units), jnp.float32),
            pltpu.VMEM((BATCH, units), bf16),
            pltpu.SemaphoreType.DMA((3,)),
            pltpu.SemaphoreType.DMA((COPIES,)),
            pltpu.SemaphoreType.DMA((COPIES,)),
        ],
        compiler_params=pltpu.CompilerParams(
            collective_id=0, has_side_effects=True, vmem_limit_bytes=56 * 1024 * 1024
        ),
    )(
        hidden_rows, norm_gain.reshape(1, width), expert_ids, capacity, route_probs,
        w_gate[0, 0], w_up[0, 0], w_down[0, 0],
    )


def solution(mesh):
    placed = (
        P(("groups", "expert", "replica"), None),
        P(),
        P(("groups", "expert", "replica"), None),
        P(),
        P(("groups", "expert", "replica"), None),
        P("expert", "replica", None, None),
        P("expert", "replica", None, None),
        P("expert", "replica", None, None),
    )
    shape = dict(mesh.shape)
    sliced = (shape["groups"], shape["expert"], shape["replica"]) == (1, 4 * CHAIN, 2)
    return jax.shard_map(
        per_device_kernel if sliced else per_device,
        mesh=mesh,
        in_specs=placed,
        out_specs=P(("groups", "expert", "replica"), None),
        check_vma=False,
    )
```

```python
import jax
import jax.numpy as jnp
from jax import lax
from jax.experimental import pallas as pl
from jax.experimental.pallas import tpu as pltpu
from jax.sharding import PartitionSpec as P

TGROUP = 8


def serve_slots(received, w_gate, w_up, w_down):
    sources, count, model_width = received.shape
    flattened = received.reshape(sources * count, model_width)
    gate_out = jnp.dot(flattened, w_gate[0, 0], preferred_element_type=jnp.float32)
    up_out = jnp.dot(flattened, w_up[0, 0], preferred_element_type=jnp.float32)
    hidden = (jax.nn.silu(gate_out) * up_out).astype(jnp.bfloat16)
    pieces = jnp.dot(hidden, w_down[0, 0], preferred_element_type=jnp.float32).astype(jnp.bfloat16)
    return pieces.reshape(sources, count, model_width)


def per_device(hidden_rows, norm_gain, expert_ids, capacity, route_probs, w_gate, w_up, w_down):
    row_count, model_width = hidden_rows.shape
    lane_count = lax.axis_size("expert")
    copies = lax.axis_size("replica")
    families = lane_count // TGROUP
    experts = families * copies
    slot_count = min(row_count, max(TGROUP, 4 * row_count // experts))
    widened = hidden_rows.astype(jnp.float32)
    scaling = lax.rsqrt(jnp.mean(widened * widened, axis=-1, keepdims=True) + 1e-05)
    normed = (widened * scaling * norm_gain).astype(jnp.bfloat16)
    assigned = expert_ids.reshape(2 * row_count)
    labels = jnp.arange(experts, dtype=jnp.int32)
    onehot = (assigned[:, None] == labels[None, :]).astype(jnp.int32)
    order_iota = jnp.arange(2 * row_count, dtype=jnp.int32)
    earlier = (order_iota[None, :] < order_iota[:, None]).astype(jnp.float32)
    counted = jnp.dot(earlier, onehot.astype(jnp.float32), preferred_element_type=jnp.float32)
    slot_rank = jnp.sum(counted.astype(jnp.int32) * onehot, axis=1)
    cap_limit = jnp.sum(onehot * capacity[None, :], axis=1)
    keep_mask = (slot_rank < cap_limit).astype(jnp.int32)
    slot_iota = jnp.arange(slot_count, dtype=jnp.int32)
    chosen = onehot.T * keep_mask[None, :]
    selection = chosen[:, None, :] * (slot_rank[None, None, :] == slot_iota[None, :, None]).astype(
        jnp.int32
    )
    selection = selection.astype(jnp.float32).reshape(experts, slot_count, row_count, 2)
    sel_rows = jnp.sum(selection, axis=3)
    weights_rows = jnp.sum(selection * route_probs[None, None, :, :], axis=3)
    outgoing = jnp.einsum(
        "ecr,rd->ecd", sel_rows.astype(jnp.bfloat16), normed, preferred_element_type=jnp.float32
    ).astype(jnp.bfloat16)
    spread = jnp.broadcast_to(
        outgoing.reshape(families, 1, copies, slot_count, model_width),
        (families, TGROUP, copies, slot_count, model_width),
    ).reshape(lane_count * copies, slot_count, model_width)
    pieces = serve_slots(
        lax.all_to_all(spread, ("expert", "replica"), split_axis=0, concat_axis=0, tiled=True),
        w_gate,
        w_up,
        w_down,
    )
    returned = lax.all_to_all(
        pieces, ("expert", "replica"), split_axis=0, concat_axis=0, tiled=True
    )
    summed = (
        returned.reshape(families, TGROUP, copies, slot_count, model_width)
        .astype(jnp.float32)
        .sum(axis=1)
        .reshape(experts, slot_count, model_width)
    )
    mixture = jnp.einsum("ecr,ecd->rd", weights_rows, summed)
    return (widened + mixture).astype(jnp.bfloat16)


CHAIN = 4
LANES = 128
HALF = 16
BLOCK = 2 * HALF
SIDE = CHAIN * BLOCK
BATCH = 2 * SIDE
STEP = 512


def rows_at(dc, dz, h=None):
    start = dc * SIDE + dz * BLOCK
    return pl.ds(start, BLOCK) if h is None else pl.ds(start + h * HALF, HALF)


def layer_kernel(
    hidden_ref, gain_ref, ids_ref, cap_ref, probs_ref, wg_hbm, wu_hbm, wd_hbm, out_ref,
    rows_buf, part_buf, pair_buf, far_buf, near_buf, chain_buf, wgu, wd, acc, hid,
    load_sem, send_sem, recv_sem,
):
    width = hidden_ref.shape[1]
    units = wd.shape[0]
    experts = cap_ref.shape[0]
    me = lax.axis_index("expert")
    core = lax.axis_index("replica")
    total = lax.axis_size("expert")
    x_side = {"expert": me + 1 - 2 * lax.rem(me, 2)}
    y_side = {"expert": me + 2 - 4 * lax.rem(lax.div(me, 2), 2)}
    sibling = {"replica": 1 - core}
    along = [{"expert": lax.rem(me + 4 * k, total)} for k in range(CHAIN)]
    near = (x_side, y_side)
    far = (y_side, x_side)

    loads = [
        pltpu.make_async_copy(src, dst, load_sem.at[n])
        for n, (src, dst) in enumerate(
            ((wg_hbm, wgu.at[pl.ds(0, units)]), (wu_hbm, wgu.at[pl.ds(units, units)]), (wd_hbm, wd))
        )
    ]
    for load in loads:
        load.start()

    barrier = pltpu.get_barrier_semaphore()
    partners = [x_side, y_side, sibling] + along[1:]
    for partner in partners:
        pl.semaphore_signal(barrier, inc=1, device_id=partner, device_id_type=pl.DeviceIdType.MESH)

    widened = hidden_ref[...].astype(jnp.float32)
    scaling = lax.rsqrt(jnp.mean(widened * widened, axis=-1, keepdims=True) + 1e-05)
    rows_buf[0, pl.ds(0, BLOCK), pl.ds(0, width)] = (widened * scaling * gain_ref[...][None, :]).astype(jnp.bfloat16)
    lane = lax.broadcasted_iota(jnp.int32, (BLOCK, LANES), 1)
    label = jnp.where(lane < LANES // 2, lane, lane - LANES // 2)
    diagonal = lax.broadcasted_iota(jnp.int32, (BLOCK, BLOCK), 0) == lax.broadcasted_iota(jnp.int32, (BLOCK, BLOCK), 1)

    def column(ref, k):
        row = ref[k : k + 1, :].astype(jnp.float32)
        return jnp.sum(jnp.where(diagonal, row, 0.0), axis=1, keepdims=True)

    first = column(ids_ref, 0).astype(jnp.int32) == label
    second = column(ids_ref, 1).astype(jnp.int32) == label
    named = jnp.where(first | second, 1.0, 0.0)
    earlier = lax.broadcasted_iota(jnp.int32, (BLOCK, BLOCK), 1) < lax.broadcasted_iota(jnp.int32, (BLOCK, BLOCK), 0)
    rank = jnp.dot(
        jnp.where(earlier, 1.0, 0.0).astype(jnp.bfloat16),
        named.astype(jnp.bfloat16),
        preferred_element_type=jnp.float32,
    )
    limit = jnp.zeros((BLOCK, LANES), jnp.float32)
    for e in range(experts):
        limit = jnp.where(label == e, cap_ref[e].astype(jnp.float32), limit)
    weight = jnp.where(first, column(probs_ref, 0), 0.0) + jnp.where(second, column(probs_ref, 1), 0.0)
    weight = jnp.where(rank < limit, weight, 0.0)
    high = weight.astype(jnp.bfloat16).astype(jnp.float32)
    rows_buf[0, pl.ds(0, BLOCK), pl.ds(width, LANES)] = jnp.where(
        lane < LANES // 2, high, weight - high
    ).astype(jnp.bfloat16)

    pl.semaphore_wait(barrier, len(partners))

    sent = {}

    def send(name, src, dst, device):
        n = len(sent)
        copy = pltpu.make_async_remote_copy(
            src_ref=src, dst_ref=dst, send_sem=send_sem.at[n], recv_sem=recv_sem.at[n],
            device_id=device, device_id_type=pl.DeviceIdType.MESH,
        )
        copy.start()
        sent[name] = copy

    def to_near(dz):
        for h in range(2):
            send(("near", dz, h), rows_buf.at[0, rows_at(0, dz, h)], rows_buf.at[1, rows_at(0, dz, h)], near[h])

    def to_far(b, dz):
        for h in range(2):
            send(("far", b, dz, h), rows_buf.at[b, rows_at(0, dz, h)], rows_buf.at[2 + b, rows_at(0, dz, h)], far[h])

    def to_sibling(batch, dz):
        send(("pair", batch, dz), rows_buf.at[batch, rows_at(0, dz)], rows_buf.at[batch, rows_at(1, dz)], sibling)

    def got(*name):
        sent[name].wait_recv()

    for k in (1, 3, 2):
        send(("along", k), rows_buf.at[0, rows_at(0, 0)], rows_buf.at[0, rows_at(0, CHAIN - k)], along[k])
    to_near(0)
    to_far(0, 0)
    to_sibling(0, 0)

    def relay_along(dz):
        got("along", CHAIN - dz)
        to_near(dz)
        to_far(0, dz)
        to_sibling(0, dz)

    def relay_near(dz):
        got("near", dz, 0)
        got("near", dz, 1)
        to_far(1, dz)
        to_sibling(1, dz)

    def relay_far(b, dz):
        got("far", b, dz, 0)
        got("far", b, dz, 1)
        to_sibling(2 + b, dz)

    def compute(batch):
        for dz in range(CHAIN):
            got("pair", batch, dz)
        acc[...] = jnp.zeros_like(acc)

        def project(n, carry):
            at = pl.ds(pl.multiple_of(n * STEP, STEP), STEP)
            acc[...] += lax.dot_general(
                wgu[:, at], rows_buf[batch, :, at], (((1,), (1,)), ((), ())), preferred_element_type=jnp.float32
            )
            return carry

        lax.fori_loop(0, width // STEP, project, 0)
        hid[...] = jnp.transpose(jax.nn.silu(acc[pl.ds(0, units), :]) * acc[pl.ds(units, units), :]).astype(jnp.bfloat16)
        mine = lax.div(me, TGROUP) * 2 + core
        lanes = lax.broadcasted_iota(jnp.int32, (BATCH, LANES), 1)
        chosen = (lanes == mine) | (lanes == mine + LANES // 2)
        tail = rows_buf[batch, :, pl.ds(width, LANES)].astype(jnp.float32)
        combine = jnp.sum(jnp.where(chosen, tail, 0.0), axis=1, keepdims=True)

        def expand(n, carry):
            at = pl.ds(pl.multiple_of(n * STEP, STEP), STEP)
            piece = jnp.dot(hid[...], wd[:, at], preferred_element_type=jnp.float32)
            part_buf[batch, :, at] = (piece * combine).astype(jnp.bfloat16)
            return carry

        lax.fori_loop(0, width // STEP, expand, 0)
        send(("sum", batch), part_buf.at[batch, pl.ds(SIDE, SIDE)], pair_buf.at[batch], sibling)

    def add_rows(batch, dst, src_ref, count):
        def body(n, carry):
            at = pl.ds(pl.multiple_of(n * HALF, HALF), HALF)
            to = pl.ds(pl.multiple_of(dst + n * HALF, HALF), HALF)
            part_buf[batch, to, :] = (
                part_buf[batch, to, :].astype(jnp.float32) + src_ref[at, :].astype(jnp.float32)
            ).astype(jnp.bfloat16)
            return carry

        lax.fori_loop(0, count, body, 0)

    def sum_pair(batch):
        got("sum", batch)
        add_rows(batch, 0, pair_buf.at[batch], SIDE // HALF)

    relay_along(1)
    relay_near(0)
    relay_along(3)
    relay_near(1)
    relay_along(2)
    relay_near(3)
    relay_near(2)
    for load in loads:
        load.wait()
    compute(0)
    compute(1)
    for dz in (0, 1, 3, 2):
        relay_far(0, dz)
    compute(2)
    for dz in (0, 1, 3, 2):
        relay_far(1, dz)
    sum_pair(2)

    def back_far(b):
        for dz in (2, 1, 3, 0):
            for h in range(2):
                send(
                    ("back_far", b, dz, h), part_buf.at[2 + b, rows_at(0, dz, h)],
                    far_buf.at[b, rows_at(0, dz, h)], far[h],
                )

    back_far(0)
    compute(3)
    sum_pair(0)
    sum_pair(1)
    sum_pair(3)
    back_far(1)
    for b in (0, 1):
        for dz in (2, 1, 3, 0):
            got("back_far", b, dz, 0)
            got("back_far", b, dz, 1)
            add_rows(b, dz * BLOCK, far_buf.at[b, rows_at(0, dz)], 2)
            if b == 1:
                for h in range(2):
                    send(
                        ("back_near", dz, h), part_buf.at[1, rows_at(0, dz, h)],
                        near_buf.at[rows_at(0, dz, h)], near[h],
                    )
    for dz in (2, 1, 3, 0):
        got("back_near", dz, 0)
        got("back_near", dz, 1)
        add_rows(0, dz * BLOCK, near_buf.at[rows_at(0, dz)], 2)
        if dz:
            send(("home", dz), part_buf.at[0, rows_at(0, dz)], chain_buf.at[dz - 1], along[dz])
    for dz in (1, 3, 2):
        got("home", dz)
    mixture = part_buf[0, pl.ds(0, BLOCK), :].astype(jnp.float32)
    for dz in range(1, CHAIN):
        mixture = mixture + chain_buf[dz - 1].astype(jnp.float32)
    out_ref[...] = (hidden_ref[...].astype(jnp.float32) + mixture).astype(jnp.bfloat16)
    for copy in sent.values():
        copy.wait_send()


COPIES = 80


def per_device_kernel(hidden_rows, norm_gain, expert_ids, capacity, route_probs, w_gate, w_up, w_down):
    row_count, width = hidden_rows.shape
    units = w_gate.shape[-1]
    vmem = pl.BlockSpec(memory_space=pltpu.VMEM)
    anywhere = pl.BlockSpec(memory_space=pl.ANY)
    bf16 = jnp.bfloat16
    return pl.pallas_call(
        layer_kernel,
        out_shape=jax.ShapeDtypeStruct((row_count, width), bf16),
        in_specs=[vmem, vmem, vmem, pl.BlockSpec(memory_space=pltpu.SMEM), vmem, anywhere, anywhere, anywhere],
        out_specs=vmem,
        scratch_shapes=[
            pltpu.VMEM((4, BATCH, width + LANES), bf16),
            pltpu.VMEM((4, BATCH, width), bf16),
            pltpu.VMEM((4, SIDE, width), bf16),
            pltpu.VMEM((2, SIDE, width), bf16),
            pltpu.VMEM((SIDE, width), bf16),
            pltpu.VMEM((CHAIN - 1, BLOCK, width), bf16),
            pltpu.VMEM((2 * units, width), bf16),
            pltpu.VMEM((units, width), bf16),
            pltpu.VMEM((2 * units, BATCH), jnp.float32),
            pltpu.VMEM((BATCH, units), bf16),
            pltpu.SemaphoreType.DMA((3,)),
            pltpu.SemaphoreType.DMA((COPIES,)),
            pltpu.SemaphoreType.DMA((COPIES,)),
        ],
        compiler_params=pltpu.CompilerParams(
            collective_id=0, has_side_effects=True, vmem_limit_bytes=56 * 1024 * 1024
        ),
    )(
        hidden_rows, norm_gain, expert_ids.T, capacity, route_probs.T,
        w_gate[0, 0].T, w_up[0, 0].T, w_down[0, 0],
    )


def solution(mesh):
    placed = (
        P(("groups", "expert", "replica"), None),
        P(),
        P(("groups", "expert", "replica"), None),
        P(),
        P(("groups", "expert", "replica"), None),
        P("expert", "replica", None, None),
        P("expert", "replica", None, None),
        P("expert", "replica", None, None),
    )
    shape = dict(mesh.shape)
    sliced = (shape["groups"], shape["expert"], shape["replica"]) == (1, 4 * CHAIN, 2)
    return jax.shard_map(
        per_device_kernel if sliced else per_device,
        mesh=mesh,
        in_specs=placed,
        out_specs=P(("groups", "expert", "replica"), None),
        check_vma=False,
    )
```

```python
import jax
import jax.numpy as jnp
from jax import lax
from jax.experimental import pallas as pl
from jax.experimental.pallas import tpu as pltpu
from jax.sharding import PartitionSpec as P

TGROUP = 8


def serve_slots(received, w_gate, w_up, w_down):
    sources, count, model_width = received.shape
    flattened = received.reshape(sources * count, model_width)
    gate_out = jnp.dot(flattened, w_gate[0, 0], preferred_element_type=jnp.float32)
    up_out = jnp.dot(flattened, w_up[0, 0], preferred_element_type=jnp.float32)
    hidden = (jax.nn.silu(gate_out) * up_out).astype(jnp.bfloat16)
    pieces = jnp.dot(hidden, w_down[0, 0], preferred_element_type=jnp.float32).astype(jnp.bfloat16)
    return pieces.reshape(sources, count, model_width)


def per_device(hidden_rows, norm_gain, expert_ids, capacity, route_probs, w_gate, w_up, w_down):
    row_count, model_width = hidden_rows.shape
    lane_count = lax.axis_size("expert")
    copies = lax.axis_size("replica")
    families = lane_count // TGROUP
    experts = families * copies
    slot_count = min(row_count, max(TGROUP, 4 * row_count // experts))
    widened = hidden_rows.astype(jnp.float32)
    scaling = lax.rsqrt(jnp.mean(widened * widened, axis=-1, keepdims=True) + 1e-05)
    normed = (widened * scaling * norm_gain).astype(jnp.bfloat16)
    assigned = expert_ids.reshape(2 * row_count)
    labels = jnp.arange(experts, dtype=jnp.int32)
    onehot = (assigned[:, None] == labels[None, :]).astype(jnp.int32)
    order_iota = jnp.arange(2 * row_count, dtype=jnp.int32)
    earlier = (order_iota[None, :] < order_iota[:, None]).astype(jnp.float32)
    counted = jnp.dot(earlier, onehot.astype(jnp.float32), preferred_element_type=jnp.float32)
    slot_rank = jnp.sum(counted.astype(jnp.int32) * onehot, axis=1)
    cap_limit = jnp.sum(onehot * capacity[None, :], axis=1)
    keep_mask = (slot_rank < cap_limit).astype(jnp.int32)
    slot_iota = jnp.arange(slot_count, dtype=jnp.int32)
    chosen = onehot.T * keep_mask[None, :]
    selection = chosen[:, None, :] * (slot_rank[None, None, :] == slot_iota[None, :, None]).astype(
        jnp.int32
    )
    selection = selection.astype(jnp.float32).reshape(experts, slot_count, row_count, 2)
    sel_rows = jnp.sum(selection, axis=3)
    weights_rows = jnp.sum(selection * route_probs[None, None, :, :], axis=3)
    outgoing = jnp.einsum(
        "ecr,rd->ecd", sel_rows.astype(jnp.bfloat16), normed, preferred_element_type=jnp.float32
    ).astype(jnp.bfloat16)
    spread = jnp.broadcast_to(
        outgoing.reshape(families, 1, copies, slot_count, model_width),
        (families, TGROUP, copies, slot_count, model_width),
    ).reshape(lane_count * copies, slot_count, model_width)
    pieces = serve_slots(
        lax.all_to_all(spread, ("expert", "replica"), split_axis=0, concat_axis=0, tiled=True),
        w_gate,
        w_up,
        w_down,
    )
    returned = lax.all_to_all(
        pieces, ("expert", "replica"), split_axis=0, concat_axis=0, tiled=True
    )
    summed = (
        returned.reshape(families, TGROUP, copies, slot_count, model_width)
        .astype(jnp.float32)
        .sum(axis=1)
        .reshape(experts, slot_count, model_width)
    )
    mixture = jnp.einsum("ecr,ecd->rd", weights_rows, summed)
    return (widened + mixture).astype(jnp.bfloat16)


CHAIN = 4
LANES = 128
HALF = 16
BLOCK = 2 * HALF
SIDE = CHAIN * BLOCK
BATCH = 2 * SIDE
STEP = 512


def rows_at(core_side, far_side, near_side, h=None):
    start = core_side * SIDE + far_side * 2 * BLOCK + near_side * BLOCK
    return pl.ds(start, BLOCK) if h is None else pl.ds(start + h * HALF, HALF)


def layer_kernel(
    hidden_ref, gain_ref, ids_ref, cap_ref, probs_ref, wg_hbm, wu_hbm, wd_hbm, out_ref,
    rows_buf, part_buf, pair_buf, far_buf, near_buf, ring_buf, wgu, wd, acc, hid,
    load_sem, send_sem, recv_sem,
):
    width = hidden_ref.shape[1]
    units = wd.shape[0]
    experts = cap_ref.shape[0]
    me = lax.axis_index("expert")
    core = lax.axis_index("replica")
    total = lax.axis_size("expert")
    x_side = {"expert": me + 1 - 2 * lax.rem(me, 2)}
    y_side = {"expert": me + 2 - 4 * lax.rem(lax.div(me, 2), 2)}
    sibling = {"replica": 1 - core}
    turn = 4 - 8 * core
    after = {"expert": lax.rem(me + total + turn, total)}
    before = {"expert": lax.rem(me + total - turn, total)}
    near = (x_side, y_side)
    far = (y_side, x_side)

    loads = [
        pltpu.make_async_copy(src, dst, load_sem.at[n])
        for n, (src, dst) in enumerate(
            ((wg_hbm, wgu.at[pl.ds(0, units)]), (wu_hbm, wgu.at[pl.ds(units, units)]), (wd_hbm, wd))
        )
    ]
    for load in loads:
        load.start()

    barrier = pltpu.get_barrier_semaphore()
    partners = [x_side, y_side, sibling, after, before]
    for partner in partners:
        pl.semaphore_signal(barrier, inc=1, device_id=partner, device_id_type=pl.DeviceIdType.MESH)

    widened = hidden_ref[...].astype(jnp.float32)
    scaling = lax.rsqrt(jnp.mean(widened * widened, axis=-1, keepdims=True) + 1e-05)
    rows_buf[0, pl.ds(0, BLOCK), pl.ds(0, width)] = (widened * scaling * gain_ref[...][None, :]).astype(jnp.bfloat16)
    lane = lax.broadcasted_iota(jnp.int32, (BLOCK, LANES), 1)
    label = jnp.where(lane < LANES // 2, lane, lane - LANES // 2)
    diagonal = lax.broadcasted_iota(jnp.int32, (BLOCK, BLOCK), 0) == lax.broadcasted_iota(jnp.int32, (BLOCK, BLOCK), 1)

    def column(ref, k):
        row = ref[k : k + 1, :].astype(jnp.float32)
        return jnp.sum(jnp.where(diagonal, row, 0.0), axis=1, keepdims=True)

    first = column(ids_ref, 0).astype(jnp.int32) == label
    second = column(ids_ref, 1).astype(jnp.int32) == label
    named = jnp.where(first | second, 1.0, 0.0)
    earlier = lax.broadcasted_iota(jnp.int32, (BLOCK, BLOCK), 1) < lax.broadcasted_iota(jnp.int32, (BLOCK, BLOCK), 0)
    rank = jnp.dot(
        jnp.where(earlier, 1.0, 0.0).astype(jnp.bfloat16),
        named.astype(jnp.bfloat16),
        preferred_element_type=jnp.float32,
    )
    limit = jnp.zeros((BLOCK, LANES), jnp.float32)
    for e in range(experts):
        limit = jnp.where(label == e, cap_ref[e].astype(jnp.float32), limit)
    weight = jnp.where(first, column(probs_ref, 0), 0.0) + jnp.where(second, column(probs_ref, 1), 0.0)
    weight = jnp.where(rank < limit, weight, 0.0)
    high = weight.astype(jnp.bfloat16).astype(jnp.float32)
    rows_buf[0, pl.ds(0, BLOCK), pl.ds(width, LANES)] = jnp.where(
        lane < LANES // 2, high, weight - high
    ).astype(jnp.bfloat16)

    pl.semaphore_wait(barrier, len(partners))

    sent = {}

    def send(name, src, dst, device):
        n = len(sent)
        copy = pltpu.make_async_remote_copy(
            src_ref=src, dst_ref=dst, send_sem=send_sem.at[n], recv_sem=recv_sem.at[n],
            device_id=device, device_id_type=pl.DeviceIdType.MESH,
        )
        copy.start()
        sent[name] = copy

    def got(*name):
        sent[name].wait_recv()

    def pass_on(s):
        if s:
            got("along", s)
        mine = rows_at(0, 0, 0)
        if s + 1 < CHAIN:
            send(("along", s + 1), rows_buf.at[s, mine], rows_buf.at[s + 1, mine], after)
        for h in range(2):
            send(("near", s, h), rows_buf.at[s, rows_at(0, 0, 0, h)], rows_buf.at[s, rows_at(0, 0, 1, h)], near[h])
        for h in range(2):
            send(("far", s, 0, h), rows_buf.at[s, rows_at(0, 0, 0, h)], rows_buf.at[s, rows_at(0, 1, 0, h)], far[h])

    def share(s, side):
        send(
            ("pair", s, side), rows_buf.at[s, pl.ds(side * 2 * BLOCK, 2 * BLOCK)],
            rows_buf.at[s, pl.ds(SIDE + side * 2 * BLOCK, 2 * BLOCK)], sibling,
        )

    def relay_near(s):
        for h in range(2):
            got("near", s, h)
            send(("far", s, 1, h), rows_buf.at[s, rows_at(0, 0, 1, h)], rows_buf.at[s, rows_at(0, 1, 1, h)], far[h])
        share(s, 0)

    def relay_far(s):
        for b in range(2):
            for h in range(2):
                got("far", s, b, h)
        share(s, 1)

    def compute(batch):
        for side in range(2):
            got("pair", batch, side)
        acc[...] = jnp.zeros_like(acc)

        def project(n, carry):
            at = pl.ds(pl.multiple_of(n * STEP, STEP), STEP)
            acc[...] += lax.dot_general(
                wgu[:, at], rows_buf[batch, :, at], (((1,), (1,)), ((), ())), preferred_element_type=jnp.float32
            )
            return carry

        lax.fori_loop(0, width // STEP, project, 0)
        hid[...] = jnp.transpose(jax.nn.silu(acc[pl.ds(0, units), :]) * acc[pl.ds(units, units), :]).astype(jnp.bfloat16)
        mine = lax.div(me, TGROUP) * 2 + core
        lanes = lax.broadcasted_iota(jnp.int32, (BATCH, LANES), 1)
        chosen = (lanes == mine) | (lanes == mine + LANES // 2)
        tail = rows_buf[batch, :, pl.ds(width, LANES)].astype(jnp.float32)
        combine = jnp.sum(jnp.where(chosen, tail, 0.0), axis=1, keepdims=True)

        def expand(n, carry):
            at = pl.ds(pl.multiple_of(n * STEP, STEP), STEP)
            piece = jnp.dot(hid[...], wd[:, at], preferred_element_type=jnp.float32)
            part_buf[batch, :, at] = (piece * combine).astype(jnp.bfloat16)
            return carry

        lax.fori_loop(0, width // STEP, expand, 0)
        send(("sum", batch), part_buf.at[batch, pl.ds(SIDE, SIDE)], pair_buf.at[batch], sibling)

    def add_rows(batch, dst, src_ref, count):
        def body(n, carry):
            at = pl.ds(pl.multiple_of(n * HALF, HALF), HALF)
            to = pl.ds(pl.multiple_of(dst + n * HALF, HALF), HALF)
            part_buf[batch, to, :] = (
                part_buf[batch, to, :].astype(jnp.float32) + src_ref[at, :].astype(jnp.float32)
            ).astype(jnp.bfloat16)
            return carry

        lax.fori_loop(0, count, body, 0)

    def sum_pair(s):
        got("sum", s)
        add_rows(s, 0, pair_buf.at[s], SIDE // HALF)
        for b in (1, 0):
            for h in range(2):
                send(
                    ("back_far", s, b, h), part_buf.at[s, rows_at(0, 1, b, h)],
                    far_buf.at[s, rows_at(0, 0, b, h)], far[h],
                )

    def sum_far(s):
        for h in range(2):
            got("back_far", s, 1, h)
            add_rows(s, BLOCK + h * HALF, far_buf.at[s, rows_at(0, 0, 1, h)], 1)
            send(("back_near", s, h), part_buf.at[s, rows_at(0, 0, 1, h)], near_buf.at[s, rows_at(0, 0, 0, h)], near[h])
        for h in range(2):
            got("back_far", s, 0, h)
            add_rows(s, h * HALF, far_buf.at[s, rows_at(0, 0, 0, h)], 1)

    def sum_near(s):
        for h in range(2):
            got("back_near", s, h)
            add_rows(s, h * HALF, near_buf.at[s, rows_at(0, 0, 0, h)], 1)
        if s != 1:
            got("home", s)
            add_rows(s, 0, ring_buf.at[s], 2)
        if s:
            last = (s + 1) % CHAIN
            send(("home", last), part_buf.at[s, rows_at(0, 0, 0)], ring_buf.at[last], after)

    pass_on(0)
    relay_near(0)
    pass_on(1)
    relay_far(0)
    relay_near(1)
    pass_on(2)
    for load in loads:
        load.wait()
    compute(0)
    relay_far(1)
    relay_near(2)
    pass_on(3)
    compute(1)
    relay_far(2)
    relay_near(3)
    sum_pair(1)
    compute(2)
    relay_far(3)
    sum_pair(2)
    sum_far(1)
    compute(3)
    sum_pair(3)
    sum_near(1)
    sum_far(2)
    sum_pair(0)
    sum_near(2)
    sum_far(3)
    sum_near(3)
    sum_far(0)
    sum_near(0)
    mixture = part_buf[0, pl.ds(0, BLOCK), :].astype(jnp.float32)
    out_ref[...] = (hidden_ref[...].astype(jnp.float32) + mixture).astype(jnp.bfloat16)
    for copy in sent.values():
        copy.wait_send()


COPIES = 66


def per_device_kernel(hidden_rows, norm_gain, expert_ids, capacity, route_probs, w_gate, w_up, w_down):
    row_count, width = hidden_rows.shape
    units = w_gate.shape[-1]
    vmem = pl.BlockSpec(memory_space=pltpu.VMEM)
    anywhere = pl.BlockSpec(memory_space=pl.ANY)
    bf16 = jnp.bfloat16
    return pl.pallas_call(
        layer_kernel,
        out_shape=jax.ShapeDtypeStruct((row_count, width), bf16),
        in_specs=[vmem, vmem, vmem, pl.BlockSpec(memory_space=pltpu.SMEM), vmem, anywhere, anywhere, anywhere],
        out_specs=vmem,
        scratch_shapes=[
            pltpu.VMEM((4, BATCH, width + LANES), bf16),
            pltpu.VMEM((4, BATCH, width), bf16),
            pltpu.VMEM((4, SIDE, width), bf16),
            pltpu.VMEM((4, 2 * BLOCK, width), bf16),
            pltpu.VMEM((4, BLOCK, width), bf16),
            pltpu.VMEM((4, BLOCK, width), bf16),
            pltpu.VMEM((2 * units, width), bf16),
            pltpu.VMEM((units, width), bf16),
            pltpu.VMEM((2 * units, BATCH), jnp.float32),
            pltpu.VMEM((BATCH, units), bf16),
            pltpu.SemaphoreType.DMA((3,)),
            pltpu.SemaphoreType.DMA((COPIES,)),
            pltpu.SemaphoreType.DMA((COPIES,)),
        ],
        compiler_params=pltpu.CompilerParams(
            collective_id=0, has_side_effects=True, vmem_limit_bytes=56 * 1024 * 1024
        ),
    )(
        hidden_rows, norm_gain, expert_ids.T, capacity, route_probs.T,
        w_gate[0, 0].T, w_up[0, 0].T, w_down[0, 0],
    )


def solution(mesh):
    placed = (
        P(("groups", "expert", "replica"), None),
        P(),
        P(("groups", "expert", "replica"), None),
        P(),
        P(("groups", "expert", "replica"), None),
        P("expert", "replica", None, None),
        P("expert", "replica", None, None),
        P("expert", "replica", None, None),
    )
    shape = dict(mesh.shape)
    sliced = (shape["groups"], shape["expert"], shape["replica"]) == (1, 4 * CHAIN, 2)
    return jax.shard_map(
        per_device_kernel if sliced else per_device,
        mesh=mesh,
        in_specs=placed,
        out_specs=P(("groups", "expert", "replica"), None),
        check_vma=False,
    )
```

```python
import jax
import jax.numpy as jnp
from jax import lax
from jax.experimental import pallas as pl
from jax.experimental.pallas import tpu as pltpu
from jax.sharding import PartitionSpec as P

TGROUP = 8


def serve_slots(received, w_gate, w_up, w_down):
    sources, count, model_width = received.shape
    flattened = received.reshape(sources * count, model_width)
    gate_out = jnp.dot(flattened, w_gate[0, 0], preferred_element_type=jnp.float32)
    up_out = jnp.dot(flattened, w_up[0, 0], preferred_element_type=jnp.float32)
    hidden = (jax.nn.silu(gate_out) * up_out).astype(jnp.bfloat16)
    pieces = jnp.dot(hidden, w_down[0, 0], preferred_element_type=jnp.float32).astype(jnp.bfloat16)
    return pieces.reshape(sources, count, model_width)


def per_device(hidden_rows, norm_gain, expert_ids, capacity, route_probs, w_gate, w_up, w_down):
    row_count, model_width = hidden_rows.shape
    lane_count = lax.axis_size("expert")
    copies = lax.axis_size("replica")
    families = lane_count // TGROUP
    experts = families * copies
    slot_count = min(row_count, max(TGROUP, 4 * row_count // experts))
    widened = hidden_rows.astype(jnp.float32)
    scaling = lax.rsqrt(jnp.mean(widened * widened, axis=-1, keepdims=True) + 1e-05)
    normed = (widened * scaling * norm_gain).astype(jnp.bfloat16)
    assigned = expert_ids.reshape(2 * row_count)
    labels = jnp.arange(experts, dtype=jnp.int32)
    onehot = (assigned[:, None] == labels[None, :]).astype(jnp.int32)
    order_iota = jnp.arange(2 * row_count, dtype=jnp.int32)
    earlier = (order_iota[None, :] < order_iota[:, None]).astype(jnp.float32)
    counted = jnp.dot(earlier, onehot.astype(jnp.float32), preferred_element_type=jnp.float32)
    slot_rank = jnp.sum(counted.astype(jnp.int32) * onehot, axis=1)
    cap_limit = jnp.sum(onehot * capacity[None, :], axis=1)
    keep_mask = (slot_rank < cap_limit).astype(jnp.int32)
    slot_iota = jnp.arange(slot_count, dtype=jnp.int32)
    chosen = onehot.T * keep_mask[None, :]
    selection = chosen[:, None, :] * (slot_rank[None, None, :] == slot_iota[None, :, None]).astype(
        jnp.int32
    )
    selection = selection.astype(jnp.float32).reshape(experts, slot_count, row_count, 2)
    sel_rows = jnp.sum(selection, axis=3)
    weights_rows = jnp.sum(selection * route_probs[None, None, :, :], axis=3)
    outgoing = jnp.einsum(
        "ecr,rd->ecd", sel_rows.astype(jnp.bfloat16), normed, preferred_element_type=jnp.float32
    ).astype(jnp.bfloat16)
    spread = jnp.broadcast_to(
        outgoing.reshape(families, 1, copies, slot_count, model_width),
        (families, TGROUP, copies, slot_count, model_width),
    ).reshape(lane_count * copies, slot_count, model_width)
    pieces = serve_slots(
        lax.all_to_all(spread, ("expert", "replica"), split_axis=0, concat_axis=0, tiled=True),
        w_gate,
        w_up,
        w_down,
    )
    returned = lax.all_to_all(
        pieces, ("expert", "replica"), split_axis=0, concat_axis=0, tiled=True
    )
    summed = (
        returned.reshape(families, TGROUP, copies, slot_count, model_width)
        .astype(jnp.float32)
        .sum(axis=1)
        .reshape(experts, slot_count, model_width)
    )
    mixture = jnp.einsum("ecr,ecd->rd", weights_rows, summed)
    return (widened + mixture).astype(jnp.bfloat16)


CHAIN = 4
LANES = 128
HALF = 16
BLOCK = 2 * HALF
SIDE = CHAIN * BLOCK
BATCH = 2 * SIDE
STEP = 1792
SPLIT = 2816


def rows_at(core_side, far_side, h, near_side, count=HALF):
    return pl.ds(core_side * SIDE + far_side * 2 * BLOCK + h * BLOCK + near_side * HALF, count)


def layer_kernel(
    hidden_ref, gain_ref, ids_ref, cap_ref, probs_ref, wg_hbm, wu_hbm, wd_hbm, out_ref,
    rows_buf, part_buf, pair_buf, far_buf, near_buf, ring_buf, wgu, wd, acc, hid,
    load_sem, send_sem, recv_sem,
):
    width = hidden_ref.shape[1]
    units = wd.shape[0]
    experts = cap_ref.shape[0]
    me = lax.axis_index("expert")
    core = lax.axis_index("replica")
    total = lax.axis_size("expert")
    x_side = {"expert": me + 1 - 2 * lax.rem(me, 2)}
    y_side = {"expert": me + 2 - 4 * lax.rem(lax.div(me, 2), 2)}
    sibling = {"replica": 1 - core}
    turn = 4 - 8 * core
    after = {"expert": lax.rem(me + total + turn, total)}
    before = {"expert": lax.rem(me + total - turn, total)}
    near = (x_side, y_side)
    far = (y_side, x_side)

    loads = [
        pltpu.make_async_copy(src, dst, load_sem.at[n])
        for n, (src, dst) in enumerate(
            ((wg_hbm, wgu.at[pl.ds(0, units)]), (wu_hbm, wgu.at[pl.ds(units, units)]), (wd_hbm, wd))
        )
    ]
    for load in loads:
        load.start()

    barrier = pltpu.get_barrier_semaphore()
    partners = [x_side, y_side, sibling, after, before]
    for partner in partners:
        pl.semaphore_signal(barrier, inc=1, device_id=partner, device_id_type=pl.DeviceIdType.MESH)

    widened = hidden_ref[...].astype(jnp.float32)
    scaling = lax.rsqrt(jnp.mean(widened * widened, axis=-1, keepdims=True) + 1e-05)
    normed = (widened * scaling * gain_ref[...][None, :]).astype(jnp.bfloat16)
    for h in range(2):
        rows_buf[0, rows_at(0, 0, h, 0), pl.ds(0, width)] = normed[h * HALF : (h + 1) * HALF]
    lane = lax.broadcasted_iota(jnp.int32, (BLOCK, LANES), 1)
    label = jnp.where(lane < LANES // 2, lane, lane - LANES // 2)
    diagonal = lax.broadcasted_iota(jnp.int32, (BLOCK, BLOCK), 0) == lax.broadcasted_iota(jnp.int32, (BLOCK, BLOCK), 1)

    def column(ref, k):
        row = ref[k : k + 1, :].astype(jnp.float32)
        return jnp.sum(jnp.where(diagonal, row, 0.0), axis=1, keepdims=True)

    first = column(ids_ref, 0).astype(jnp.int32) == label
    second = column(ids_ref, 1).astype(jnp.int32) == label
    named = jnp.where(first | second, 1.0, 0.0)
    earlier = lax.broadcasted_iota(jnp.int32, (BLOCK, BLOCK), 1) < lax.broadcasted_iota(jnp.int32, (BLOCK, BLOCK), 0)
    rank = jnp.dot(
        jnp.where(earlier, 1.0, 0.0).astype(jnp.bfloat16),
        named.astype(jnp.bfloat16),
        preferred_element_type=jnp.float32,
    )
    limit = jnp.zeros((BLOCK, LANES), jnp.float32)
    for e in range(experts):
        limit = jnp.where(label == e, cap_ref[e].astype(jnp.float32), limit)
    weight = jnp.where(first, column(probs_ref, 0), 0.0) + jnp.where(second, column(probs_ref, 1), 0.0)
    weight = jnp.where(rank < limit, weight, 0.0)
    high = weight.astype(jnp.bfloat16).astype(jnp.float32)
    tail = jnp.where(lane < LANES // 2, high, weight - high).astype(jnp.bfloat16)
    for h in range(2):
        rows_buf[0, rows_at(0, 0, h, 0), pl.ds(width, LANES)] = tail[h * HALF : (h + 1) * HALF]

    pl.semaphore_wait(barrier, len(partners))

    sent = {}

    def send(name, src, dst, device):
        n = len(sent)
        copy = pltpu.make_async_remote_copy(
            src_ref=src, dst_ref=dst, send_sem=send_sem.at[n], recv_sem=recv_sem.at[n],
            device_id=device, device_id_type=pl.DeviceIdType.MESH,
        )
        copy.start()
        sent[name] = copy

    def got(*name):
        sent[name].wait_recv()

    z_first = pl.ds(0, SPLIT)
    near_first = pl.ds(SPLIT, width + LANES - SPLIT)

    def relay(name, s, src, dst, device, columns, to=None):
        send(name, rows_buf.at[s, src, columns], rows_buf.at[s if to is None else to, dst, columns], device)

    def pass_on(s):
        for h in range(2):
            own = rows_at(0, 0, h, 0)
            if s:
                got("along", s, h)
            if s + 1 < CHAIN:
                relay(("along", s + 1, h), s, own, own, after, z_first, s + 1)
        for h in range(2):
            relay(("near", s, h), s, rows_at(0, 0, h, 0), rows_at(0, 0, h, 1), near[h], z_first)
        for h in range(2):
            relay(("far", s, 0, h), s, rows_at(0, 0, h, 0), rows_at(0, 1, h, 0), far[h], z_first)

    def start_near():
        for h in range(2):
            relay(("near_one", h), 0, rows_at(0, 0, h, 0), rows_at(0, 0, h, 1), near[h], near_first)

    def pass_two(s):
        if s:
            got("along_two", s)
        else:
            for h in range(2):
                got("near_one", h)
        both = pl.ds(0, 2 * BLOCK)
        if s + 1 < CHAIN:
            relay(("along_two", s + 1), s, both, both, after, near_first, s + 1)
        for h in range(2):
            relay(("far_two", s, h), s, rows_at(0, 0, h, 0, BLOCK), rows_at(0, 1, h, 0, BLOCK), far[h], near_first)

    def share(s, side):
        send(
            ("pair", s, side), rows_buf.at[s, pl.ds(side * 2 * BLOCK, 2 * BLOCK)],
            rows_buf.at[s, pl.ds(SIDE + side * 2 * BLOCK, 2 * BLOCK)], sibling,
        )

    def relay_near(s):
        for h in range(2):
            got("near", s, h)
            relay(("far", s, 1, h), s, rows_at(0, 0, h, 1), rows_at(0, 1, h, 1), far[h], z_first)
        share(s, 0)

    def relay_far(s):
        for h in range(2):
            for b in range(2):
                got("far", s, b, h)
            got("far_two", s, h)
        share(s, 1)

    def compute(batch):
        for side in range(2):
            got("pair", batch, side)
        acc[...] = jnp.zeros_like(acc)

        def project(n, carry):
            at = pl.ds(pl.multiple_of(n * STEP, STEP), STEP)
            acc[...] += lax.dot_general(
                wgu[:, at], rows_buf[batch, :, at], (((1,), (1,)), ((), ())), preferred_element_type=jnp.float32
            )
            return carry

        lax.fori_loop(0, width // STEP, project, 0)
        hid[...] = jnp.transpose(jax.nn.silu(acc[pl.ds(0, units), :]) * acc[pl.ds(units, units), :]).astype(jnp.bfloat16)
        mine = lax.div(me, TGROUP) * 2 + core
        lanes = lax.broadcasted_iota(jnp.int32, (BATCH, LANES), 1)
        chosen = (lanes == mine) | (lanes == mine + LANES // 2)
        tail = rows_buf[batch, :, pl.ds(width, LANES)].astype(jnp.float32)
        combine = jnp.sum(jnp.where(chosen, tail, 0.0), axis=1, keepdims=True)

        def expand(n, carry):
            at = pl.ds(pl.multiple_of(n * STEP, STEP), STEP)
            piece = jnp.dot(hid[...], wd[:, at], preferred_element_type=jnp.float32)
            part_buf[batch, :, at] = (piece * combine).astype(jnp.bfloat16)
            return carry

        lax.fori_loop(0, width // STEP, expand, 0)
        send(("sum", batch), part_buf.at[batch, pl.ds(SIDE, SIDE)], pair_buf.at[batch], sibling)

    def add_rows(batch, dst, src_ref, count, columns):
        def body(n, carry):
            at = pl.ds(pl.multiple_of(n * HALF, HALF), HALF)
            to = pl.ds(pl.multiple_of(dst + n * HALF, HALF), HALF)
            part_buf[batch, to, columns] = (
                part_buf[batch, to, columns].astype(jnp.float32) + src_ref[at, columns].astype(jnp.float32)
            ).astype(jnp.bfloat16)
            return carry

        lax.fori_loop(0, count, body, 0)

    last_near = pl.ds(SPLIT, width - SPLIT)

    def give(name, s, src, buf, to, dst, device, columns):
        send(name, part_buf.at[s, src, columns], buf.at[to, dst, columns], device)

    def sum_pair(s):
        got("sum", s)
        add_rows(s, 0, pair_buf.at[s], SIDE // HALF, pl.ds(0, width))
        for h in range(2):
            give(
                ("back_far_two", s, h), s, rows_at(0, 1, h, 0, BLOCK), far_buf, s, rows_at(0, 0, h, 0, BLOCK),
                far[h], last_near,
            )
        for b in (1, 0):
            for h in range(2):
                give(("back_far", s, b, h), s, rows_at(0, 1, h, b), far_buf, s, rows_at(0, 0, h, b), far[h], z_first)

    def sum_far(s):
        for h in range(2):
            got("back_far_two", s, h)
            add_rows(s, h * BLOCK, far_buf.at[s, pl.ds(h * BLOCK, BLOCK)], 2, last_near)
        if s != 1:
            got("home_two", s)
            add_rows(s, 0, ring_buf.at[s], 4, last_near)
        if s:
            following = (s + 1) % CHAIN
            both = pl.ds(0, 2 * BLOCK)
            give(("home_two", following), s, both, ring_buf, following, both, after, last_near)
        else:
            for h in range(2):
                give(
                    ("back_near_one", h), 0, rows_at(0, 0, h, 1), near_buf, 0, pl.ds(h * HALF, HALF), near[h], last_near
                )
        for h in range(2):
            got("back_far", s, 1, h)
            add_rows(s, h * BLOCK + HALF, far_buf.at[s, rows_at(0, 0, h, 1)], 1, z_first)
            give(("back_near", s, h), s, rows_at(0, 0, h, 1), near_buf, s, pl.ds(h * HALF, HALF), near[h], z_first)
        for h in range(2):
            got("back_far", s, 0, h)
            add_rows(s, h * BLOCK, far_buf.at[s, rows_at(0, 0, h, 0)], 1, z_first)

    def sum_near(s):
        for h in range(2):
            own = rows_at(0, 0, h, 0)
            got("back_near", s, h)
            add_rows(s, h * BLOCK, near_buf.at[s, pl.ds(h * HALF, HALF)], 1, z_first)
            if s != 1:
                got("home", s, h)
                add_rows(s, h * BLOCK, ring_buf.at[s, own], 1, z_first)
            if s:
                following = (s + 1) % CHAIN
                give(("home", following, h), s, own, ring_buf, following, own, after, z_first)
        if s == 0:
            for h in range(2):
                got("back_near_one", h)
                add_rows(s, h * BLOCK, near_buf.at[s, pl.ds(h * HALF, HALF)], 1, last_near)

    start_near()
    pass_on(0)
    pass_two(0)
    relay_near(0)
    pass_on(1)
    pass_two(1)
    relay_far(0)
    relay_near(1)
    pass_on(2)
    pass_two(2)
    for load in loads:
        load.wait()
    compute(0)
    relay_far(1)
    relay_near(2)
    pass_on(3)
    pass_two(3)
    compute(1)
    relay_far(2)
    relay_near(3)
    sum_pair(1)
    compute(2)
    relay_far(3)
    sum_pair(2)
    compute(3)
    sum_far(1)
    sum_pair(3)
    sum_near(1)
    sum_far(2)
    sum_pair(0)
    sum_near(2)
    sum_far(3)
    sum_near(3)
    sum_far(0)
    sum_near(0)
    for h in range(2):
        mine = pl.ds(h * HALF, HALF)
        mixture = part_buf[0, rows_at(0, 0, h, 0), :].astype(jnp.float32)
        out_ref[mine, :] = (hidden_ref[mine, :].astype(jnp.float32) + mixture).astype(jnp.bfloat16)
    for copy in sent.values():
        copy.wait_send()


COPIES = 98


def per_device_kernel(hidden_rows, norm_gain, expert_ids, capacity, route_probs, w_gate, w_up, w_down):
    row_count, width = hidden_rows.shape
    units = w_gate.shape[-1]
    vmem = pl.BlockSpec(memory_space=pltpu.VMEM)
    anywhere = pl.BlockSpec(memory_space=pl.ANY)
    bf16 = jnp.bfloat16
    return pl.pallas_call(
        layer_kernel,
        out_shape=jax.ShapeDtypeStruct((row_count, width), bf16),
        in_specs=[vmem, vmem, vmem, pl.BlockSpec(memory_space=pltpu.SMEM), vmem, anywhere, anywhere, anywhere],
        out_specs=vmem,
        scratch_shapes=[
            pltpu.VMEM((4, BATCH, width + LANES), bf16),
            pltpu.VMEM((4, BATCH, width), bf16),
            pltpu.VMEM((4, SIDE, width), bf16),
            pltpu.VMEM((4, 2 * BLOCK, width), bf16),
            pltpu.VMEM((4, BLOCK, width), bf16),
            pltpu.VMEM((4, 2 * BLOCK, width), bf16),
            pltpu.VMEM((2 * units, width), bf16),
            pltpu.VMEM((units, width), bf16),
            pltpu.VMEM((2 * units, BATCH), jnp.float32),
            pltpu.VMEM((BATCH, units), bf16),
            pltpu.SemaphoreType.DMA((3,)),
            pltpu.SemaphoreType.DMA((COPIES,)),
            pltpu.SemaphoreType.DMA((COPIES,)),
        ],
        compiler_params=pltpu.CompilerParams(
            collective_id=0, has_side_effects=True, vmem_limit_bytes=56 * 1024 * 1024
        ),
    )(
        hidden_rows, norm_gain, expert_ids.T, capacity, route_probs.T,
        w_gate[0, 0].T, w_up[0, 0].T, w_down[0, 0],
    )


def solution(mesh):
    placed = (
        P(("groups", "expert", "replica"), None),
        P(),
        P(("groups", "expert", "replica"), None),
        P(),
        P(("groups", "expert", "replica"), None),
        P("expert", "replica", None, None),
        P("expert", "replica", None, None),
        P("expert", "replica", None, None),
    )
    shape = dict(mesh.shape)
    sliced = (shape["groups"], shape["expert"], shape["replica"]) == (1, 4 * CHAIN, 2)
    return jax.shard_map(
        per_device_kernel if sliced else per_device,
        mesh=mesh,
        in_specs=placed,
        out_specs=P(("groups", "expert", "replica"), None),
        check_vma=False,
    )
```

```python
import jax
import jax.numpy as jnp
from jax import lax
from jax.experimental import pallas as pl
from jax.experimental.pallas import tpu as pltpu
from jax.sharding import PartitionSpec as P

TGROUP = 8


def serve_slots(received, w_gate, w_up, w_down):
    sources, count, model_width = received.shape
    flattened = received.reshape(sources * count, model_width)
    gate_out = jnp.dot(flattened, w_gate[0, 0], preferred_element_type=jnp.float32)
    up_out = jnp.dot(flattened, w_up[0, 0], preferred_element_type=jnp.float32)
    hidden = (jax.nn.silu(gate_out) * up_out).astype(jnp.bfloat16)
    pieces = jnp.dot(hidden, w_down[0, 0], preferred_element_type=jnp.float32).astype(jnp.bfloat16)
    return pieces.reshape(sources, count, model_width)


def per_device(hidden_rows, norm_gain, expert_ids, capacity, route_probs, w_gate, w_up, w_down):
    row_count, model_width = hidden_rows.shape
    lane_count = lax.axis_size("expert")
    copies = lax.axis_size("replica")
    families = lane_count // TGROUP
    experts = families * copies
    slot_count = min(row_count, max(TGROUP, 4 * row_count // experts))
    widened = hidden_rows.astype(jnp.float32)
    scaling = lax.rsqrt(jnp.mean(widened * widened, axis=-1, keepdims=True) + 1e-05)
    normed = (widened * scaling * norm_gain).astype(jnp.bfloat16)
    assigned = expert_ids.reshape(2 * row_count)
    labels = jnp.arange(experts, dtype=jnp.int32)
    onehot = (assigned[:, None] == labels[None, :]).astype(jnp.int32)
    order_iota = jnp.arange(2 * row_count, dtype=jnp.int32)
    earlier = (order_iota[None, :] < order_iota[:, None]).astype(jnp.float32)
    counted = jnp.dot(earlier, onehot.astype(jnp.float32), preferred_element_type=jnp.float32)
    slot_rank = jnp.sum(counted.astype(jnp.int32) * onehot, axis=1)
    cap_limit = jnp.sum(onehot * capacity[None, :], axis=1)
    keep_mask = (slot_rank < cap_limit).astype(jnp.int32)
    slot_iota = jnp.arange(slot_count, dtype=jnp.int32)
    chosen = onehot.T * keep_mask[None, :]
    selection = chosen[:, None, :] * (slot_rank[None, None, :] == slot_iota[None, :, None]).astype(
        jnp.int32
    )
    selection = selection.astype(jnp.float32).reshape(experts, slot_count, row_count, 2)
    sel_rows = jnp.sum(selection, axis=3)
    weights_rows = jnp.sum(selection * route_probs[None, None, :, :], axis=3)
    outgoing = jnp.einsum(
        "ecr,rd->ecd", sel_rows.astype(jnp.bfloat16), normed, preferred_element_type=jnp.float32
    ).astype(jnp.bfloat16)
    spread = jnp.broadcast_to(
        outgoing.reshape(families, 1, copies, slot_count, model_width),
        (families, TGROUP, copies, slot_count, model_width),
    ).reshape(lane_count * copies, slot_count, model_width)
    pieces = serve_slots(
        lax.all_to_all(spread, ("expert", "replica"), split_axis=0, concat_axis=0, tiled=True),
        w_gate,
        w_up,
        w_down,
    )
    returned = lax.all_to_all(
        pieces, ("expert", "replica"), split_axis=0, concat_axis=0, tiled=True
    )
    summed = (
        returned.reshape(families, TGROUP, copies, slot_count, model_width)
        .astype(jnp.float32)
        .sum(axis=1)
        .reshape(experts, slot_count, model_width)
    )
    mixture = jnp.einsum("ecr,ecd->rd", weights_rows, summed)
    return (widened + mixture).astype(jnp.bfloat16)


CHAIN = 4
LANES = 128
HALF = 16
BLOCK = 2 * HALF
SIDE = CHAIN * BLOCK
BATCH = 2 * SIDE
STEP = 1792
SPLIT = 2816


def rows_at(core_side, far_side, h, near_side, count=HALF):
    return pl.ds(core_side * SIDE + far_side * 2 * BLOCK + h * BLOCK + near_side * HALF, count)


def layer_kernel(
    hidden_ref, gain_ref, ids_ref, cap_ref, probs_ref, wg_hbm, wu_hbm, wd_hbm, out_ref,
    rows_buf, part_buf, pair_buf, far_buf, near_buf, ring_buf, wgu, wd, acc, hid,
    load_sem, send_sem, recv_sem,
):
    width = hidden_ref.shape[1]
    units = wd.shape[0]
    experts = cap_ref.shape[0]
    me = lax.axis_index("expert")
    core = lax.axis_index("replica")
    total = lax.axis_size("expert")
    x_side = {"expert": me + 1 - 2 * lax.rem(me, 2)}
    y_side = {"expert": me + 2 - 4 * lax.rem(lax.div(me, 2), 2)}
    sibling = {"replica": 1 - core}
    turn = 4 - 8 * core
    after = {"expert": lax.rem(me + total + turn, total)}
    before = {"expert": lax.rem(me + total - turn, total)}
    near = (x_side, y_side)
    far = (y_side, x_side)

    loads = [
        pltpu.make_async_copy(src, dst, load_sem.at[n])
        for n, (src, dst) in enumerate(
            ((wg_hbm, wgu.at[pl.ds(0, units)]), (wu_hbm, wgu.at[pl.ds(units, units)]), (wd_hbm, wd))
        )
    ]
    for load in loads:
        load.start()

    barrier = pltpu.get_barrier_semaphore()
    partners = [x_side, y_side, sibling, after, before]
    for partner in partners:
        pl.semaphore_signal(barrier, inc=1, device_id=partner, device_id_type=pl.DeviceIdType.MESH)

    widened = hidden_ref[...].astype(jnp.float32)
    scaling = lax.rsqrt(jnp.mean(widened * widened, axis=-1, keepdims=True) + 1e-05)
    normed = (widened * scaling * gain_ref[...][None, :]).astype(jnp.bfloat16)
    for h in range(2):
        rows_buf[0, rows_at(0, 0, h, 0), pl.ds(0, width)] = normed[h * HALF : (h + 1) * HALF]
    lane = lax.broadcasted_iota(jnp.int32, (BLOCK, LANES), 1)
    label = jnp.where(lane < LANES // 2, lane, lane - LANES // 2)
    diagonal = lax.broadcasted_iota(jnp.int32, (BLOCK, BLOCK), 0) == lax.broadcasted_iota(jnp.int32, (BLOCK, BLOCK), 1)

    def column(ref, k):
        row = ref[k : k + 1, :].astype(jnp.float32)
        return jnp.sum(jnp.where(diagonal, row, 0.0), axis=1, keepdims=True)

    first = column(ids_ref, 0).astype(jnp.int32) == label
    second = column(ids_ref, 1).astype(jnp.int32) == label
    named = jnp.where(first | second, 1.0, 0.0)
    earlier = lax.broadcasted_iota(jnp.int32, (BLOCK, BLOCK), 1) < lax.broadcasted_iota(jnp.int32, (BLOCK, BLOCK), 0)
    rank = jnp.dot(
        jnp.where(earlier, 1.0, 0.0).astype(jnp.bfloat16),
        named.astype(jnp.bfloat16),
        preferred_element_type=jnp.float32,
    )
    limit = jnp.zeros((BLOCK, LANES), jnp.float32)
    for e in range(experts):
        limit = jnp.where(label == e, cap_ref[e].astype(jnp.float32), limit)
    weight = jnp.where(first, column(probs_ref, 0), 0.0) + jnp.where(second, column(probs_ref, 1), 0.0)
    weight = jnp.where(rank < limit, weight, 0.0)
    high = weight.astype(jnp.bfloat16).astype(jnp.float32)
    tail = jnp.where(lane < LANES // 2, high, weight - high).astype(jnp.bfloat16)
    for h in range(2):
        rows_buf[0, rows_at(0, 0, h, 0), pl.ds(width, LANES)] = tail[h * HALF : (h + 1) * HALF]

    pl.semaphore_wait(barrier, len(partners))

    sent = {}

    def send(name, src, dst, device):
        n = len(sent)
        copy = pltpu.make_async_remote_copy(
            src_ref=src, dst_ref=dst, send_sem=send_sem.at[n], recv_sem=recv_sem.at[n],
            device_id=device, device_id_type=pl.DeviceIdType.MESH,
        )
        copy.start()
        sent[name] = copy

    def got(*name):
        sent[name].wait_recv()

    z_first = pl.ds(0, SPLIT)
    near_first = pl.ds(SPLIT, width + LANES - SPLIT)

    def relay(name, s, src, dst, device, columns, to=None):
        send(name, rows_buf.at[s, src, columns], rows_buf.at[s if to is None else to, dst, columns], device)

    def pass_on(s):
        for h in range(2):
            own = rows_at(0, 0, h, 0)
            if s:
                got("along", s, h)
            if s + 1 < CHAIN:
                relay(("along", s + 1, h), s, own, own, after, z_first, s + 1)
        for h in range(2):
            relay(("near", s, h), s, rows_at(0, 0, h, 0), rows_at(0, 0, h, 1), near[h], z_first)

    def pass_far(s):
        for h in range(2):
            relay(("far", s, 0, h), s, rows_at(0, 0, h, 0), rows_at(0, 1, h, 0), far[h], z_first)

    def start_near():
        for h in range(2):
            relay(("near_one", h), 0, rows_at(0, 0, h, 0), rows_at(0, 0, h, 1), near[h], near_first)

    def pass_two(s):
        if s:
            got("along_two", s)
        else:
            for h in range(2):
                got("near_one", h)
        both = pl.ds(0, 2 * BLOCK)
        if s + 1 < CHAIN:
            relay(("along_two", s + 1), s, both, both, after, near_first, s + 1)
        for h in range(2):
            relay(("far_two", s, h), s, rows_at(0, 0, h, 0, BLOCK), rows_at(0, 1, h, 0, BLOCK), far[h], near_first)

    def share(s, side):
        send(
            ("pair", s, side), rows_buf.at[s, pl.ds(side * 2 * BLOCK, 2 * BLOCK)],
            rows_buf.at[s, pl.ds(SIDE + side * 2 * BLOCK, 2 * BLOCK)], sibling,
        )

    def relay_near(s):
        for h in range(2):
            got("near", s, h)
            relay(("far", s, 1, h), s, rows_at(0, 0, h, 1), rows_at(0, 1, h, 1), far[h], z_first)
        share(s, 0)

    def relay_far(s):
        for h in range(2):
            for b in range(2):
                got("far", s, b, h)
            got("far_two", s, h)
        share(s, 1)

    def compute(batch):
        for side in range(2):
            got("pair", batch, side)
        acc[...] = jnp.zeros_like(acc)

        def project(n, carry):
            at = pl.ds(pl.multiple_of(n * STEP, STEP), STEP)
            acc[...] += lax.dot_general(
                wgu[:, at], rows_buf[batch, :, at], (((1,), (1,)), ((), ())), preferred_element_type=jnp.float32
            )
            return carry

        lax.fori_loop(0, width // STEP, project, 0)
        hid[...] = jnp.transpose(jax.nn.silu(acc[pl.ds(0, units), :]) * acc[pl.ds(units, units), :]).astype(jnp.bfloat16)
        mine = lax.div(me, TGROUP) * 2 + core
        lanes = lax.broadcasted_iota(jnp.int32, (BATCH, LANES), 1)
        chosen = (lanes == mine) | (lanes == mine + LANES // 2)
        tail = rows_buf[batch, :, pl.ds(width, LANES)].astype(jnp.float32)
        combine = jnp.sum(jnp.where(chosen, tail, 0.0), axis=1, keepdims=True)

        for n in range(width // STEP):
            at = pl.ds(n * STEP, STEP)
            piece = jnp.dot(hid[...], wd[:, at], preferred_element_type=jnp.float32)
            part_buf[batch, :, at] = (piece * combine).astype(jnp.bfloat16)
            send(("sum", batch, n), part_buf.at[batch, pl.ds(SIDE, SIDE), at], pair_buf.at[batch, :, at], sibling)

    def add_rows(batch, dst, src_ref, count, columns):
        def body(n, carry):
            at = pl.ds(pl.multiple_of(n * HALF, HALF), HALF)
            to = pl.ds(pl.multiple_of(dst + n * HALF, HALF), HALF)
            part_buf[batch, to, columns] = (
                part_buf[batch, to, columns].astype(jnp.float32) + src_ref[at, columns].astype(jnp.float32)
            ).astype(jnp.bfloat16)
            return carry

        lax.fori_loop(0, count, body, 0)

    last_near = pl.ds(SPLIT, width - SPLIT)

    def give(name, s, src, buf, to, dst, device, columns):
        send(name, part_buf.at[s, src, columns], buf.at[to, dst, columns], device)

    def sum_pair(s):
        for n in range(width // STEP):
            got("sum", s, n)
            add_rows(s, 0, pair_buf.at[s], SIDE // HALF, pl.ds(n * STEP, STEP))
        for h in range(2):
            give(
                ("back_far_two", s, h), s, rows_at(0, 1, h, 0, BLOCK), far_buf, s, rows_at(0, 0, h, 0, BLOCK),
                far[h], last_near,
            )
        for b in (1, 0):
            for h in range(2):
                give(("back_far", s, b, h), s, rows_at(0, 1, h, b), far_buf, s, rows_at(0, 0, h, b), far[h], z_first)

    def sum_far(s):
        for h in range(2):
            got("back_far_two", s, h)
            add_rows(s, h * BLOCK, far_buf.at[s, pl.ds(h * BLOCK, BLOCK)], 2, last_near)
        if s != 1:
            got("home_two", s)
            add_rows(s, 0, ring_buf.at[s], 4, last_near)
        if s:
            following = (s + 1) % CHAIN
            both = pl.ds(0, 2 * BLOCK)
            give(("home_two", following), s, both, ring_buf, following, both, after, last_near)
        else:
            for h in range(2):
                give(
                    ("back_near_one", h), 0, rows_at(0, 0, h, 1), near_buf, 0, pl.ds(h * HALF, HALF), near[h], last_near
                )
        for h in range(2):
            got("back_far", s, 1, h)
            add_rows(s, h * BLOCK + HALF, far_buf.at[s, rows_at(0, 0, h, 1)], 1, z_first)
            give(("back_near", s, h), s, rows_at(0, 0, h, 1), near_buf, s, pl.ds(h * HALF, HALF), near[h], z_first)
        for h in range(2):
            got("back_far", s, 0, h)
            add_rows(s, h * BLOCK, far_buf.at[s, rows_at(0, 0, h, 0)], 1, z_first)

    def sum_near(s):
        for h in range(2):
            own = rows_at(0, 0, h, 0)
            got("back_near", s, h)
            add_rows(s, h * BLOCK, near_buf.at[s, pl.ds(h * HALF, HALF)], 1, z_first)
            if s != 1:
                got("home", s, h)
                add_rows(s, h * BLOCK, ring_buf.at[s, own], 1, z_first)
            if s:
                following = (s + 1) % CHAIN
                give(("home", following, h), s, own, ring_buf, following, own, after, z_first)
        if s == 0:
            for h in range(2):
                got("back_near_one", h)
                add_rows(s, h * BLOCK, near_buf.at[s, pl.ds(h * HALF, HALF)], 1, last_near)

    start_near()
    pass_on(0)
    pass_two(0)
    pass_far(0)
    relay_near(0)
    pass_on(1)
    pass_two(1)
    pass_far(1)
    relay_far(0)
    relay_near(1)
    pass_on(2)
    pass_two(2)
    pass_far(2)
    for load in loads:
        load.wait()
    compute(0)
    relay_far(1)
    relay_near(2)
    pass_on(3)
    pass_two(3)
    pass_far(3)
    compute(1)
    relay_far(2)
    relay_near(3)
    sum_pair(1)
    compute(2)
    relay_far(3)
    sum_pair(2)
    compute(3)
    sum_far(1)
    sum_pair(3)
    sum_near(1)
    sum_far(2)
    sum_pair(0)
    sum_near(2)
    sum_far(3)
    sum_near(3)
    sum_far(0)
    sum_near(0)
    for h in range(2):
        mine = pl.ds(h * HALF, HALF)
        mixture = part_buf[0, rows_at(0, 0, h, 0), :].astype(jnp.float32)
        out_ref[mine, :] = (hidden_ref[mine, :].astype(jnp.float32) + mixture).astype(jnp.bfloat16)
    for copy in sent.values():
        copy.wait_send()


COPIES = 102


def per_device_kernel(hidden_rows, norm_gain, expert_ids, capacity, route_probs, w_gate, w_up, w_down):
    row_count, width = hidden_rows.shape
    units = w_gate.shape[-1]
    vmem = pl.BlockSpec(memory_space=pltpu.VMEM)
    anywhere = pl.BlockSpec(memory_space=pl.ANY)
    bf16 = jnp.bfloat16
    return pl.pallas_call(
        layer_kernel,
        out_shape=jax.ShapeDtypeStruct((row_count, width), bf16),
        in_specs=[vmem, vmem, vmem, pl.BlockSpec(memory_space=pltpu.SMEM), vmem, anywhere, anywhere, anywhere],
        out_specs=vmem,
        scratch_shapes=[
            pltpu.VMEM((4, BATCH, width + LANES), bf16),
            pltpu.VMEM((4, BATCH, width), bf16),
            pltpu.VMEM((4, SIDE, width), bf16),
            pltpu.VMEM((4, 2 * BLOCK, width), bf16),
            pltpu.VMEM((4, BLOCK, width), bf16),
            pltpu.VMEM((4, 2 * BLOCK, width), bf16),
            pltpu.VMEM((2 * units, width), bf16),
            pltpu.VMEM((units, width), bf16),
            pltpu.VMEM((2 * units, BATCH), jnp.float32),
            pltpu.VMEM((BATCH, units), bf16),
            pltpu.SemaphoreType.DMA((3,)),
            pltpu.SemaphoreType.DMA((COPIES,)),
            pltpu.SemaphoreType.DMA((COPIES,)),
        ],
        compiler_params=pltpu.CompilerParams(
            collective_id=0, has_side_effects=True, vmem_limit_bytes=56 * 1024 * 1024
        ),
    )(
        hidden_rows, norm_gain, expert_ids.T, capacity, route_probs.T,
        w_gate[0, 0].T, w_up[0, 0].T, w_down[0, 0],
    )


def solution(mesh):
    placed = (
        P(("groups", "expert", "replica"), None),
        P(),
        P(("groups", "expert", "replica"), None),
        P(),
        P(("groups", "expert", "replica"), None),
        P("expert", "replica", None, None),
        P("expert", "replica", None, None),
        P("expert", "replica", None, None),
    )
    shape = dict(mesh.shape)
    sliced = (shape["groups"], shape["expert"], shape["replica"]) == (1, 4 * CHAIN, 2)
    return jax.shard_map(
        per_device_kernel if sliced else per_device,
        mesh=mesh,
        in_specs=placed,
        out_specs=P(("groups", "expert", "replica"), None),
        check_vma=False,
    )
```
